256 devices in a mesh: pool: 32 (over x_hi, z, core), tp: 8 (over x_lo, y).
Axes of the slice: x: 4 (x_hi: 2, x_lo: 2; x = x_hi * 2 + x_lo), y: 4, z: 8, core: 2. Of those that a mesh axis runs over, the one named last changes fastest.
Arguments:
- queries: bfloat16 [32768, 8192], P('pool', 'tp'), may hold values from -10 to 10
- keys: bfloat16 [32768, 1024], P('pool', 'tp'), may hold values from -6 to 6
- values: bfloat16 [32768, 1024], P('pool', 'tp'), may hold values from -6 to 6
- start_pages: int32 [32], P('pool'), may hold values from 0 to 255
- owners: int32 [32, 16, 1], P('pool'), may hold values from 0 to 31; in each aligned block of 16 rows (0 to 15, 16 to 31, ..., all dimensions but the last counted through in order) at most 2 rows name the same one
Outputs:
- mixed: bfloat16 [32768, 8192], P('pool', 'tp')
- store: bfloat16 [2048, 64, 2, 1024], P(('pool', 'tp'))
The draws below stay inside these ranges and needn't reach their ends.
Inputs may be any that keep to these rules, and one draw needn't show every extreme that they name: `owners`: in each group at most 2 pages name the same owner, and some group has exactly 2 pages with one owner.
All inputs are finite; a program needn't handle non-finite values.
Results may differ from the reference program's by a relative error of at most 0.011.
Values may be sent and summed in bfloat16 or wider, within the bound.
A program may use at most 128 MiB of HBM per device.

```python
import math
import jax
import jax.numpy as jnp
import numpy as np
from jax import lax

H = 64
KVH = 8
HD = 128
PAGE = 64
CAP = 2
TOK_GROUP = 1024
TOKENS = 32768
PAGES_GROUP = 16
SLOTS = 64
STORE_ROWS = 2048
N_POOL = 32


def draw_keys(key, part):
    key = jax.random.fold_in(key, 21)
    drawn = jax.random.truncated_normal(key, -6.0, 6.0, (TOKENS, KVH * HD), jnp.float32)
    return drawn.astype(jnp.bfloat16)


def draw_queries(key, part):
    key = jax.random.fold_in(key, 33)
    drawn = jax.random.truncated_normal(key, -6.0, 6.0, (TOKENS, H * HD), jnp.float32)
    return drawn.astype(jnp.bfloat16)


def plant(entries, rng, low, high):
    longest = entries.shape.index(max(entries.shape))
    spots = []
    for shift in (0, 1):
        where = [jax.random.randint(jax.random.fold_in(rng, axis), (), 0, length) for axis, length in enumerate(entries.shape)]
        where[longest] = (where[longest] + shift) % entries.shape[longest]
        spots.append(tuple(where))
    return entries.at[spots[0]].set(low).at[spots[1]].set(high)


def shard_levels(stream_key, dims, shards, low, high):
    gain, own = 1.0, jax.random.fold_in(stream_key, 6)
    for dim, parts in shards:
        draws = jnp.exp(jax.random.uniform(jax.random.fold_in(own, dim), (parts,), jnp.float32, low / len(shards), high / len(shards)))
        gain = gain * jnp.repeat(draws, dims[dim] // parts).reshape([-1 if axis == dim else 1 for axis in range(len(dims))])
    return gain


def assign_block(own_key, own, number, rows, amount, top, reach, slope):
    sequence = jax.random.permutation(own_key, amount)
    packed, common = portions_of(amount, rows * top, reach, slope, True), portions_of(amount, rows * top, reach, slope, False)
    places = jnp.arange(amount)

    def named(tallies, turn):
        used = int((tallies > 0).sum())
        fixed = max(1, used // 4)
        passed = fixed + (places - fixed + turn * (used - fixed)) % max(1, amount - fixed)
        return jnp.zeros((amount,), jnp.int32).at[sequence[jnp.where(places < fixed, places, passed)]].set(jnp.asarray(tallies, jnp.int32))

    tallies = jnp.where(number % 4 == 0, named(packed, number // 4), named(common, number - number // 4 - 1))
    mixed = jax.random.permutation(jax.random.fold_in(own, 3), amount)
    giver, receiver = mixed[0:amount // 2 * 2:2], mixed[1:amount // 2 * 2:2]
    margin = jnp.minimum(tallies[giver] - 1, reach - tallies[receiver]) // 2
    margin = jnp.where((giver == sequence[0]) | (receiver == sequence[0]) | (tallies[receiver] == 0), 0, jnp.maximum(margin, 0))
    passed = jax.random.randint(jax.random.fold_in(own, 4), (amount // 2,), 0, 1 << 20) % (margin + 1)
    tallies = tallies.at[giver].add(-passed).at[receiver].add(passed)
    labels = jnp.searchsorted(jnp.cumsum(tallies), jnp.arange(rows * top), side="right").astype(jnp.int32)
    table = labels.reshape(top, rows).T
    table = table[jax.random.permutation(jax.random.fold_in(own, 1), rows)]
    turn = jax.random.randint(jax.random.fold_in(own, 2), (rows, 1), 0, top)
    return jnp.take_along_axis(table, (jnp.arange(top)[None, :] + turn) % top, axis=1)


def portions_of(number_of, total, limit, skew, full):
    weights = [(1 << 20) // math.isqrt(rank ** skew) + 1 for rank in range(1, number_of + 1)]
    largest = limit if full else min(limit, max(-(-total // number_of), total * weights[0] // sum(weights)))
    least = 1 if total - largest >= number_of - 1 else 0
    counts, surplus = [largest] + [least] * (number_of - 1), total - largest - least * (number_of - 1)
    while surplus > 0:
        movable = [i for i in range(1, number_of) if counts[i] < largest] or [i for i in range(1, number_of) if counts[i] < limit]
        pool, left = sum([weights[i] for i in movable]), surplus
        for i in movable:
            more = min(limit - counts[i], max(1, left * weights[i] // pool), surplus)
            counts[i] = counts[i] + more
            surplus = surplus - more
    return np.array(counts)


def bell_draw(stream_key, dims, spread, reach, split=(), kind=jnp.bfloat16):
    values = jax.random.normal(stream_key, dims, jnp.float32) * spread
    if len(split) > 0:
        values = shard_levels(stream_key, dims, split, -0.22, 0.18) * values
    return jnp.clip(values, min=-reach, max=reach).astype(kind)


def setup_inputs(seed: int = 0) -> dict:
    key_list = jax.random.split(jax.random.key(seed), 6)
    queries = draw_queries(jax.random.fold_in(key_list[5], 71), 0)
    keys = draw_keys(jax.random.fold_in(key_list[5], 71), 0)
    values = bell_draw(key_list[2], (TOKENS, KVH * HD), 1.0, 6.0, ((0, 32), (1, 8)))
    start_pages = plant(jax.random.randint(key_list[3], (N_POOL,), 0, 256), jax.random.fold_in(key_list[3], 1), 0, 255).astype(jnp.int32)
    owners_keys = jax.random.split(jax.random.fold_in(key_list[4], 1), N_POOL * PAGES_GROUP // PAGES_GROUP)
    owners_turns = jax.random.permutation(jax.random.fold_in(key_list[4], 3), N_POOL * PAGES_GROUP // PAGES_GROUP)
    owners = jax.vmap(lambda own, number: assign_block(jax.random.fold_in(key_list[4], 2), own, number, PAGES_GROUP, N_POOL, 1, CAP, 2))(owners_keys, owners_turns).reshape((N_POOL, PAGES_GROUP, 1))
    return dict(queries=queries, keys=keys, values=values, start_pages=start_pages, owners=owners)


ROPE_THETA = 1000000.0

def rotate(tensor, position):
    half_dim = tensor.shape[-1] // 2
    inverse = ROPE_THETA ** (-(jnp.arange(half_dim, dtype=jnp.float32) * 2.0) / (2.0 * half_dim))
    angles = position[:, None] * inverse[None, :]
    cosine = jnp.concatenate([jnp.cos(angles), jnp.cos(angles)], axis=-1)
    sine = jnp.concatenate([jnp.sin(angles), jnp.sin(angles)], axis=-1)
    first = tensor[..., :half_dim]
    second = tensor[..., half_dim:]
    turned = jnp.concatenate([-second, first], axis=-1)
    extended = (tensor.shape[0],) + (1,) * (tensor.ndim - 2) + (tensor.shape[-1],)
    return tensor * cosine.reshape(extended) + turned * sine.reshape(extended)

def attend(query_rot, key_rot, value_heads):
    length = query_rot.shape[0]
    block = min(512, length)
    scale = 1.0 / math.sqrt(query_rot.shape[-1])
    results = []
    for block_index in range(length // block):
        finish = (block_index + 1) * block
        query_block = query_rot[block_index * block:finish].astype(jnp.float32)
        key_block = key_rot[:finish].astype(jnp.float32)
        value_block = value_heads[:finish].astype(jnp.float32)
        scores = jnp.einsum('qkgd,skd->kgqs', query_block, key_block) * scale
        query_pos = block_index * block + jnp.arange(block)
        key_pos = jnp.arange(finish)
        allowed = key_pos[None, :] <= query_pos[:, None]
        scores = jnp.where(allowed, scores, jnp.float32(-1e+30))
        highest = lax.optimization_barrier(jnp.max(scores, axis=-1, keepdims=True))
        weights = jnp.exp(scores - highest)
        total = lax.optimization_barrier(jnp.sum(weights, axis=-1, keepdims=True))
        probs = (weights / total).astype(jnp.bfloat16)
        output = jnp.einsum('kgqs,skd->qkgd', probs.astype(jnp.float32), value_block)
        results.append(output.astype(jnp.bfloat16).reshape(block, -1))
    return jnp.concatenate(results, axis=0)

def reference(queries, keys, values, start_pages, owners):
    group_q = queries.reshape(N_POOL, TOK_GROUP, KVH, H // KVH, HD)
    group_k = keys.reshape(N_POOL, TOK_GROUP, KVH, HD)
    group_v = values.reshape(N_POOL, TOK_GROUP, KVH, HD)

    def one_group(inputs):
        query_part, key_part, value_part, start = inputs
        position = (PAGE * start + jnp.arange(TOK_GROUP)).astype(jnp.float32)
        query_rot = rotate(query_part.astype(jnp.float32), position).astype(jnp.bfloat16)
        key_rot = rotate(key_part.astype(jnp.float32), position).astype(jnp.bfloat16)
        return (attend(query_rot, key_rot, value_part), key_rot)
    attended, key_rot = lax.map(one_group, (group_q, group_k, group_v, start_pages))
    mixed = attended.reshape(TOKENS, H * HD)
    pieces = jnp.stack([key_rot.reshape(N_POOL, TOK_GROUP, KVH * HD), values.reshape(N_POOL, TOK_GROUP, KVH * HD)], axis=2)
    pieces = pieces.reshape(N_POOL * PAGES_GROUP, PAGE, 2, KVH * HD)
    owner_ids = owners[:, :, 0]
    earlier = jnp.arange(PAGES_GROUP)[None, :] < jnp.arange(PAGES_GROUP)[:, None]
    same_owner = owner_ids[:, :, None] == owner_ids[:, None, :]
    rank = lax.optimization_barrier(jnp.sum(jnp.logical_and(same_owner, earlier[None]), axis=2)).astype(jnp.int32)
    target = owner_ids * SLOTS + jnp.arange(N_POOL, dtype=jnp.int32)[:, None] * CAP + rank
    store = jnp.zeros((STORE_ROWS, PAGE, 2, KVH * HD), jnp.bfloat16)
    store = store.at[target.reshape(-1)].set(pieces)
    return (mixed, store)
```

```python
import functools
import math

import jax
import jax.numpy as jnp
import numpy as np
from jax import lax
from jax.experimental import pallas as pl
from jax.experimental.pallas import tpu as pltpu
from jax.sharding import PartitionSpec as P

HD = 128
PAGE = 64
ROPE_THETA = 1000000.0
MESH = pl.DeviceIdType.MESH
NZ = 8
NP = 16
T = 1024
NH = 8
C = 4
AHEAD = 2
LATE = 4
R = 2 * PAGE // C
BQ = 256
NQ = T // BQ
F32 = jnp.float32
BF16 = jnp.bfloat16


def dev(xh, z, c, xl, y):
    return (xh * 16 + z * 2 + c, xl * 4 + y)


def dot_t(a, b):
    return lax.dot_general(a, b, (((1,), (1,)), ((), ())), preferred_element_type=F32)


def main_kernel(inv_ref, start_ref, owners_ref, q_hbm, k_hbm, v_hbm, mixed_hbm, land, *scratch):
    (qbuf, kbuf, vbuf, mbuf, cos_t, sin_t, krot, vext, tbl, tbl_in, tbl_s,
     xs, d3o, d4o, in_sem, tl_sem, t_send, t_recv, r_send, r_recv, d3_send, d3_recv,
     d4_send, d4_recv, p_send, p_recv, x_send, l_recv, out_sem) = scratch[:29]
    blocks = scratch[29:]
    raw = blocks[0:C]
    ra = (blocks[C:2 * C], blocks[2 * C:3 * C])
    rb = (blocks[3 * C:4 * C], blocks[4 * C:5 * C])

    p_idx, t_idx = lax.axis_index("pool"), lax.axis_index("tp")
    xh, z, c = p_idx // 16, (p_idx // 2) % 8, p_idx % 2
    xl, y = t_idx // 4, t_idx % 4
    edge = 1 - (xl - xh) * (xl - xh)
    is_edge = xl == xh
    other = 1 - xh
    pxh, pxl = xh + edge * (1 - 2 * xh), xl + edge * (1 - 2 * xl)

    k_in = pltpu.make_async_copy(k_hbm, kbuf, in_sem.at[0])
    v_in = pltpu.make_async_copy(v_hbm, vbuf, in_sem.at[1])
    q_in = pltpu.make_async_copy(q_hbm, qbuf, in_sem.at[2])
    k_in.start()
    v_in.start()
    q_in.start()

    bar = pltpu.get_barrier_semaphore()

    def greet(*place):
        pl.semaphore_signal(bar, inc=1, device_id=dev(*place), device_id_type=MESH)

    for n in (1, 7, 2, 6):
        greet(xh, (z + n) % NZ, c, xl, y)

    @pl.when(is_edge)
    def _():
        for n in (0, 1, 7, 2, 6):
            greet(pxh, (z + n) % NZ, c, pxl, y)

    for half in range(2):
        xhd, xld = half + edge * (xh - half), xh + edge * (half - xh)
        for y2 in range(4):
            for c2 in range(2):
                here = is_edge & (half == xl) & (y2 == y) & (c2 == c)

                @pl.when(jnp.logical_not(here))
                def _():
                    greet(xhd, z, c2, xld, y2)

    own = [owners_ref[q] for q in range(NP)]
    lane = lax.broadcasted_iota(jnp.int32, (8, 128), 1)
    table = jnp.full((8, 128), -1, jnp.int32)
    for q in range(NP):
        rank = jnp.int32(0)
        for e in range(q):
            rank = rank + jnp.where(own[e] == own[q], 1, 0)
        table = jnp.where(lane == own[q] * 2 + rank, q, table)
    tbl[...] = table

    inv = inv_ref[...]
    base = start_ref[0] * PAGE
    page_pos = (base + PAGE * lax.broadcasted_iota(jnp.int32, (NP, HD), 0)).astype(F32)
    in_pos = lax.broadcasted_iota(jnp.int32, (PAGE, HD), 0).astype(F32)
    ang_p = page_pos * inv
    ang_i = in_pos * inv
    cos_p, sin_p, cos_i, sin_i = jnp.cos(ang_p), jnp.sin(ang_p), jnp.cos(ang_i), jnp.sin(ang_i)
    sign = jnp.where(lax.broadcasted_iota(jnp.int32, (PAGE, HD), 1) < HD // 2, -1.0, 1.0).astype(F32)
    row = lax.broadcasted_iota(jnp.int32, (2 * PAGE, 2 * PAGE), 0)
    col = lax.broadcasted_iota(jnp.int32, (2 * PAGE, 2 * PAGE), 1)
    weave = (col == (row // 2) + PAGE * (row % 2)).astype(BF16)
    k_in.wait()
    v_in.wait()
    for q in range(NP):
        rows = slice(q * PAGE, (q + 1) * PAGE)
        cos_q = cos_p[q:q + 1] * cos_i - sin_p[q:q + 1] * sin_i
        sin_q = (sin_p[q:q + 1] * cos_i + cos_p[q:q + 1] * sin_i) * sign
        cos_t[rows] = cos_q
        sin_t[rows] = sin_q
        k = kbuf[rows].astype(F32)
        kr = (k * cos_q + pltpu.roll(k, HD // 2, 1) * sin_q).astype(BF16)
        krot[rows] = kr
        v = vbuf[rows]
        both = jnp.dot(weave, jnp.concatenate([kr, v], axis=0), preferred_element_type=F32).astype(BF16)
        for k_ in range(C):
            raw[k_][q] = both[k_ * R:(k_ + 1) * R]
        vext[rows, 0:HD] = v
        vext[rows, HD:] = jnp.ones((PAGE, HD), BF16)

    pl.semaphore_wait(bar, 20 + 4 * edge)

    t_copies = []
    for e, n in enumerate((1, 7, 2, 6)):
        t_copies.append(pltpu.make_async_remote_copy(
            src_ref=tbl, dst_ref=tbl_in.at[e], send_sem=t_send.at[e], recv_sem=t_recv.at[e],
            device_id=dev(xh, (z + n) % NZ, c, xl, y), device_id_type=MESH))
    own_tbl = pltpu.make_async_copy(tbl, tbl_s.at[0], tl_sem.at[0])

    def raw_copy(stage, k, d):
        return pltpu.make_async_remote_copy(
            src_ref=raw[k] if stage == 0 else ra[d][k], dst_ref=ra[d][k] if stage == 0 else rb[d][k],
            send_sem=r_send.at[stage, k, d], recv_sem=r_recv.at[stage, k, d],
            device_id=dev(xh, (z + (1, 7)[d]) % NZ, c, xl, y), device_id_type=MESH)

    def d3_copy(k, d, half):
        swap = edge * (xh if half == 0 else 1 - xh)
        to = half + swap * (xh - half)
        return pltpu.make_async_remote_copy(
            src_ref=d3o.at[d, k, half], dst_ref=xs.at[k, (5, 3)[d], to],
            send_sem=d3_send.at[k, d, half], recv_sem=d3_recv.at[k, d, to],
            device_id=dev(xh + swap * (1 - 2 * xh), (z + (1, 7)[d]) % NZ, c, xl + swap * (1 - 2 * xl), y),
            device_id_type=MESH)

    def d4_copy(k, d):
        swap = 0 if d == 0 else edge
        to = xh if d == 0 else other + edge * (xh - other)
        return pltpu.make_async_remote_copy(
            src_ref=d4o.at[d, k], dst_ref=xs.at[k, 4, to],
            send_sem=d4_send.at[k, d], recv_sem=d4_recv.at[k, to],
            device_id=dev(xh + swap * (1 - 2 * xh), (z + (2, 6)[d]) % NZ, c, xl + swap * (1 - 2 * xl), y),
            device_id_type=MESH)

    def pass_copy(k, dz):
        return pltpu.make_async_remote_copy(
            src_ref=xs.at[k, dz, 2], dst_ref=xs.at[k, dz, xh],
            send_sem=p_send.at[k, dz], recv_sem=p_recv.at[k, dz],
            device_id=dev(pxh, z, c, pxl, y), device_id_type=MESH)

    def to_owner(k, dz, second):
        zs = (z + dz) % NZ
        y2 = zs // 2
        if second:
            half, xhd, xld = other, other + edge * (xh - other), xh + edge * (other - xh)
            hxl = xl + edge * (1 - 2 * xl)
        else:
            half, xhd, xld, hxl = xh, xh, xh, xl
        for c2 in range(2):
            src = xs.at[k, dz, half, c2]
            at = (((zs % 2) * 2 + c) * 8 + hxl * 4 + y) * 2
            dst = land.at[pl.ds(at, 2), pl.ds(k * R, R)]

            def remote():
                pltpu.make_async_remote_copy(
                    src_ref=src, dst_ref=dst, send_sem=x_send, recv_sem=l_recv,
                    device_id=dev(xhd, z, c2, xld, y2), device_id_type=MESH).start()

            if second:
                remote()
            else:
                here = is_edge & (y2 == y) & (c2 == c)

                @pl.when(here)
                def _():
                    pltpu.make_async_copy(src, dst, l_recv).start()

                pl.when(jnp.logical_not(here))(remote)

    def pick(ref, which, slot):
        idx = tbl_s[which, 0, slot]
        page = ref[jnp.maximum(idx, 0)]
        return jnp.where(idx >= 0, page, jnp.zeros_like(page))

    def extract(ref, which, k, dz):
        for half in range(2):
            swap = edge * (xh if half == 0 else 1 - xh)
            to = half + swap * (2 - half)
            for c2 in range(2):
                for r in range(2):
                    xs[k, dz, to, c2, r] = pick(ref, which, half * 32 + z * 4 + c2 * 2 + r)

        @pl.when(is_edge)
        def _():
            pass_copy(k, dz).start()

        to_owner(k, dz, False)

    def passed(k, dz):
        @pl.when(is_edge)
        def _():
            pass_copy(k, dz).wait_recv()

        to_owner(k, dz, True)

    def ev_tables():
        for e, cp in enumerate(t_copies):
            cp.wait()
            pltpu.make_async_copy(tbl_in.at[e], tbl_s.at[e + 1], tl_sem.at[e + 1]).start()
        for e in range(4):
            pltpu.make_async_copy(tbl_in.at[e], tbl_s.at[e + 1], tl_sem.at[e + 1]).wait()

    def ev_own(k):
        extract(raw[k], 0, k, 0)

    def ev_one(k):
        for d in range(2):
            raw_copy(0, k, d).wait_recv()
            raw_copy(1, k, d).start()
        if k + AHEAD < C:
            for d in range(2):
                raw_copy(0, k + AHEAD, d).start()
        for d in range(2):
            extract(ra[d][k], 1 + d, k, (7, 1)[d])

    def ev_two(k):
        for d in range(2):
            raw_copy(1, k, d).wait_recv()
            n3, n4 = ((1, 2), (7, 6))[d]
            half4 = xh if d == 0 else other
            for c2 in range(2):
                for r in range(2):
                    d4o[d, k, c2, r] = pick(rb[d][k], 3 + d, half4 * 32 + ((z + n4) % NZ) * 4 + c2 * 2 + r)
            d4_copy(k, d).start()
            for half in range(2):
                for c2 in range(2):
                    for r in range(2):
                        d3o[d, k, half, c2, r] = pick(rb[d][k], 3 + d, half * 32 + ((z + n3) % NZ) * 4 + c2 * 2 + r)
                d3_copy(k, d, half).start()
        for d in range(2):
            extract(rb[d][k], 3 + d, k, (6, 2)[d])

    def ev_pass1(k):
        for dz in (0, 7, 1):
            passed(k, dz)

    def ev_far(k):
        for dz in (6, 2):
            passed(k, dz)
        for d in range(2):
            for half in range(2):
                d3_copy_in(k, d, half)
            to_owner(k, (5, 3)[d], False)
            to_owner(k, (5, 3)[d], True)
        for half in range(2):
            d4_copy_in(k, half)
        to_owner(k, 4, False)
        to_owner(k, 4, True)

    def d3_copy_in(k, d, half):
        landed = xs.at[k, (5, 3)[d], half]
        pltpu.make_async_copy(landed, landed, d3_recv.at[k, d, half]).wait()

    def d4_copy_in(k, half):
        landed = xs.at[k, 4, half]
        pltpu.make_async_copy(landed, landed, d4_recv.at[k, half]).wait()

    scale = math.log2(math.e) / math.sqrt(HD)

    def attend(h, i):
        rows = slice(i * BQ, (i + 1) * BQ)
        cols = pl.ds(pl.multiple_of(h * HD, HD), HD)
        q = qbuf[rows, cols].astype(F32)
        qr = (q * cos_t[rows] + pltpu.roll(q, HD // 2, 1) * sin_t[rows]).astype(BF16)
        s_d = dot_t(qr, krot[rows])
        keep = (lax.broadcasted_iota(jnp.int32, (BQ, BQ), 1) <= lax.broadcasted_iota(jnp.int32, (BQ, BQ), 0))
        s_d = jnp.where(keep, s_d, -1e30)
        top = jnp.max(s_d, axis=1, keepdims=True)
        if i > 0:
            s_f = dot_t(qr, krot[0:i * BQ])
            top = jnp.maximum(top, jnp.max(s_f, axis=1, keepdims=True))
        w_d = jnp.exp2((s_d - top) * scale).astype(BF16)
        out = jnp.dot(w_d, vext[rows], preferred_element_type=F32)
        if i > 0:
            w_f = jnp.exp2((s_f - top) * scale).astype(BF16)
            out = out + jnp.dot(w_f, vext[0:i * BQ], preferred_element_type=F32)
        mbuf[rows, cols] = (out[:, 0:HD] / out[:, HD:]).astype(BF16)

    own_tbl.start()
    for k in range(AHEAD):
        for d in range(2):
            raw_copy(0, k, d).start()
        if k == 0:
            for cp in t_copies:
                cp.start()
    own_tbl.wait()
    q_in.wait()

    events = [functools.partial(ev_own, 0), ev_tables]
    for r in range(C + 2):
        if r < C:
            events.append(functools.partial(ev_one, r))
            if r + 1 < C:
                events.append(functools.partial(ev_own, r + 1))
        if 0 <= r - 1 < C:
            events.append(functools.partial(ev_two, r - 1))
            events.append(functools.partial(ev_pass1, r - 1))
        if 0 <= r - 2 < C:
            events.append(functools.partial(ev_far, r - 2))
    units = NH * NQ
    at_step = {}
    for n, e in enumerate(events[:-LATE]):
        at_step.setdefault(n * units // (len(events) - LATE), []).append(e)

    def unit(s, carry):
        for n, es in at_step.items():
            @pl.when(s == n)
            def _():
                for e in es:
                    e()
        h, i = s // NQ, s % NQ
        for j in range(NQ):
            @pl.when(i == j)
            def _():
                attend(h, j)
        return carry

    lax.fori_loop(0, units, unit, 0)
    out = pltpu.make_async_copy(mbuf, mixed_hbm, out_sem)
    out.start()
    for e in events[-LATE:]:
        e()
    out.wait()
    for k in range(C):
        for d in range(2):
            raw_copy(0, k, d).wait_send()
            raw_copy(1, k, d).wait_send()
            d4_copy(k, d).wait_send()
            for half in range(2):
                d3_copy(k, d, half).wait_send()

        @pl.when(is_edge)
        def _():
            for dz in (0, 7, 1, 6, 2):
                pass_copy(k, dz).wait_send()
    whole = land.at[pl.ds(0, 60)]
    pltpu.make_async_copy(whole, whole, x_send).wait()

    @pl.when(jnp.logical_not(is_edge))
    def _():
        rest = land.at[pl.ds(60, 4)]
        pltpu.make_async_copy(rest, rest, x_send).wait()

    pltpu.make_async_copy(land, land, l_recv).wait()


def layout_kernel(land, mixed_in, store, mixed, lbuf, mbuf, sem, msem):
    parts = 4
    rows = T // parts
    ins, outs = [], []
    for g in range(4):
        ins.append(pltpu.make_async_copy(land.at[pl.ds(g * 16, 16)], lbuf.at[pl.ds(g * 16, 16)], sem.at[0, g]))
        ins.append(pltpu.make_async_copy(
            mixed_in.at[pl.ds(g * rows, rows)], mbuf.at[pl.ds(g * rows, rows)], msem.at[0, g]))
    for cp in ins:
        cp.start()
    for g in range(4):
        ins[2 * g].wait()
        for h in range(8):
            for r in range(2):
                outs.append(pltpu.make_async_copy(
                    lbuf.at[(g * 8 + h) * 2 + r], store.at[g * 2 + r, :, :, pl.ds(h * HD, HD)],
                    sem.at[1 + h * 2 + r, g]))
                outs[-1].start()
        ins[2 * g + 1].wait()
        outs.append(pltpu.make_async_copy(
            mbuf.at[pl.ds(g * rows, rows)], mixed.at[pl.ds(g * rows, rows)], msem.at[1, g]))
        outs[-1].start()
    for cp in outs:
        cp.wait()


def on_device(queries, keys, values, start_pages, owners):
    half = HD // 2
    inv = ROPE_THETA ** (-(np.arange(half, dtype=np.float64) * 2.0) / HD)
    inv = jnp.asarray(np.concatenate([inv, inv]).astype(np.float32).reshape(1, HD))
    anys = pl.BlockSpec(memory_space=pl.ANY)
    smem = pl.BlockSpec(memory_space=pltpu.SMEM)
    vm = lambda *s: pltpu.VMEM(s, BF16)
    dma = lambda *s: pltpu.SemaphoreType.DMA(s) if s else pltpu.SemaphoreType.DMA
    blocks = [vm(NP, R, HD)] * (5 * C)
    mixed, land = pl.pallas_call(
        main_kernel,
        out_shape=(jax.ShapeDtypeStruct((T, NH * HD), BF16), jax.ShapeDtypeStruct((64, 2 * PAGE, HD), BF16)),
        in_specs=[pl.BlockSpec(memory_space=pltpu.VMEM), smem, smem, anys, anys, anys],
        out_specs=(anys, anys),
        scratch_shapes=[
            vm(T, NH * HD), vm(T, HD), vm(T, HD), vm(T, NH * HD),
            pltpu.VMEM((T, HD), F32), pltpu.VMEM((T, HD), F32), vm(T, HD), vm(T, 2 * HD),
            pltpu.VMEM((8, 128), jnp.int32), pltpu.VMEM((4, 8, 128), jnp.int32), pltpu.SMEM((5, 8, 128), jnp.int32),
            vm(C, NZ, 3, 2, 2, R, HD), vm(2, C, 2, 2, 2, R, HD), vm(2, C, 2, 2, R, HD),
            dma(3), dma(5),
            dma(4), dma(4),
            dma(2, C, 2), dma(2, C, 2), dma(C, 2, 2), dma(C, 2, 2), dma(C, 2), dma(C, 2), dma(C, NZ), dma(C, NZ),
            dma(), dma(), dma(),
        ] + blocks,
        compiler_params=pltpu.CompilerParams(
            collective_id=0, has_side_effects=True, vmem_limit_bytes=56 << 20),
    )(inv, start_pages, owners.reshape(NP), queries, keys, values)
    store, mixed = pl.pallas_call(
        layout_kernel,
        out_shape=(jax.ShapeDtypeStruct((8, PAGE, 2, 8 * HD), BF16), jax.ShapeDtypeStruct((T, NH * HD), BF16)),
        in_specs=[anys, anys],
        out_specs=(anys, anys),
        scratch_shapes=[vm(64, PAGE, 2, HD), vm(T, NH * HD), dma(17, 4), dma(2, 4)],
        compiler_params=pltpu.CompilerParams(vmem_limit_bytes=24 << 20),
    )(land.reshape(64, PAGE, 2, HD), mixed)
    return (mixed, store)


def solution(mesh):
    return jax.shard_map(
        on_device,
        mesh=mesh,
        in_specs=(
            P("pool", "tp"),
            P("pool", "tp"),
            P("pool", "tp"),
            P("pool"),
            P("pool", None, None),
        ),
        out_specs=(P("pool", "tp"), P(("pool", "tp"), None, None, None)),
        check_vma=False,
    )
```

```python
import functools
import math

import jax
import jax.numpy as jnp
import numpy as np
from jax import lax
from jax.experimental import pallas as pl
from jax.experimental.pallas import tpu as pltpu
from jax.sharding import PartitionSpec as P

HD = 128
PAGE = 64
ROPE_THETA = 1000000.0
MESH = pl.DeviceIdType.MESH
NZ = 8
NP = 16
T = 1024
NH = 8
C = 8
AHEAD = 3
R = 2 * PAGE // C
BQ = 256
HG = 4
NQ = T // BQ
F32 = jnp.float32
BF16 = jnp.bfloat16


def dev(xh, z, c, xl, y):
    return (xh * 16 + z * 2 + c, xl * 4 + y)


def dot_t(a, b):
    return lax.dot_general(a, b, (((1,), (1,)), ((), ())), preferred_element_type=F32)


def main_kernel(inv_ref, start_ref, owners_ref, q_hbm, k_hbm, v_hbm, mixed_hbm, land, *scratch):
    (qbuf, kbuf, vbuf, mbuf, cos_t, sin_t, krot, vext, tbl, tbl_in, tbl_s,
     xs, d3o, d4o, in_sem, tl_sem, t_send, t_recv, r_send, r_recv, d3_send, d3_recv,
     d4_send, d4_recv, p_send, p_recv, x_send, l_recv, out_sem) = scratch[:29]
    blocks = scratch[29:]
    raw = blocks[0:C]
    ra = (blocks[C:2 * C], blocks[2 * C:3 * C])
    rb = (blocks[3 * C:4 * C], blocks[4 * C:5 * C])

    p_idx, t_idx = lax.axis_index("pool"), lax.axis_index("tp")
    xh, z, c = p_idx // 16, (p_idx // 2) % 8, p_idx % 2
    xl, y = t_idx // 4, t_idx % 4
    edge = 1 - (xl - xh) * (xl - xh)
    is_edge = xl == xh
    other = 1 - xh
    pxh, pxl = xh + edge * (1 - 2 * xh), xl + edge * (1 - 2 * xl)

    k_in = pltpu.make_async_copy(k_hbm, kbuf, in_sem.at[0])
    v_in = pltpu.make_async_copy(v_hbm, vbuf, in_sem.at[1])
    q_in = pltpu.make_async_copy(q_hbm, qbuf, in_sem.at[2])
    k_in.start()
    v_in.start()

    bar = pltpu.get_barrier_semaphore()

    def greet(*place):
        pl.semaphore_signal(bar, inc=1, device_id=dev(*place), device_id_type=MESH)

    for n in (1, 7, 2, 6):
        greet(xh, (z + n) % NZ, c, xl, y)

    @pl.when(is_edge)
    def _():
        for n in (0, 1, 7, 2, 6):
            greet(pxh, (z + n) % NZ, c, pxl, y)

    for half in range(2):
        xhd, xld = half + edge * (xh - half), xh + edge * (half - xh)
        for y2 in range(4):
            for c2 in range(2):
                here = is_edge & (half == xl) & (y2 == y) & (c2 == c)

                @pl.when(jnp.logical_not(here))
                def _():
                    greet(xhd, z, c2, xld, y2)

    own = [owners_ref[q] for q in range(NP)]
    lane = lax.broadcasted_iota(jnp.int32, (8, 128), 1)
    table = jnp.full((8, 128), -1, jnp.int32)
    for q in range(NP):
        rank = jnp.int32(0)
        for e in range(q):
            rank = rank + jnp.where(own[e] == own[q], 1, 0)
        table = jnp.where(lane == own[q] * 2 + rank, q, table)
    tbl[...] = table

    inv = inv_ref[...]
    base = start_ref[0] * PAGE
    page_pos = (base + PAGE * lax.broadcasted_iota(jnp.int32, (NP, HD), 0)).astype(F32)
    in_pos = lax.broadcasted_iota(jnp.int32, (PAGE, HD), 0).astype(F32)
    ang_p = page_pos * inv
    ang_i = in_pos * inv
    cos_p, sin_p, cos_i, sin_i = jnp.cos(ang_p), jnp.sin(ang_p), jnp.cos(ang_i), jnp.sin(ang_i)
    sign = jnp.where(lax.broadcasted_iota(jnp.int32, (PAGE, HD), 1) < HD // 2, -1.0, 1.0).astype(F32)
    row = lax.broadcasted_iota(jnp.int32, (2 * PAGE, 2 * PAGE), 0)
    col = lax.broadcasted_iota(jnp.int32, (2 * PAGE, 2 * PAGE), 1)
    weave = (col == (row // 2) + PAGE * (row % 2)).astype(BF16)
    k_in.wait()
    v_in.wait()
    q_in.start()
    for q in range(NP):
        rows = slice(q * PAGE, (q + 1) * PAGE)
        cos_q = cos_p[q:q + 1] * cos_i - sin_p[q:q + 1] * sin_i
        sin_q = (sin_p[q:q + 1] * cos_i + cos_p[q:q + 1] * sin_i) * sign
        cos_t[rows] = cos_q
        sin_t[rows] = sin_q
        k = kbuf[rows].astype(F32)
        kr = (k * cos_q + pltpu.roll(k, HD // 2, 1) * sin_q).astype(BF16)
        krot[rows] = kr
        v = vbuf[rows]
        both = jnp.dot(weave, jnp.concatenate([kr, v], axis=0), preferred_element_type=F32).astype(BF16)
        for k_ in range(C):
            raw[k_][q] = both[k_ * R:(k_ + 1) * R]
        vext[rows, 0:HD] = v
        vext[rows, HD:] = jnp.ones((PAGE, HD), BF16)

    pl.semaphore_wait(bar, 20 + 4 * edge)

    t_copies = []
    for e, n in enumerate((1, 7, 2, 6)):
        t_copies.append(pltpu.make_async_remote_copy(
            src_ref=tbl, dst_ref=tbl_in.at[e], send_sem=t_send.at[e], recv_sem=t_recv.at[e],
            device_id=dev(xh, (z + n) % NZ, c, xl, y), device_id_type=MESH))
    own_tbl = pltpu.make_async_copy(tbl, tbl_s.at[0], tl_sem.at[0])

    def raw_copy(stage, k, d):
        return pltpu.make_async_remote_copy(
            src_ref=raw[k] if stage == 0 else ra[d][k], dst_ref=ra[d][k] if stage == 0 else rb[d][k],
            send_sem=r_send.at[stage, k, d], recv_sem=r_recv.at[stage, k, d],
            device_id=dev(xh, (z + (1, 7)[d]) % NZ, c, xl, y), device_id_type=MESH)

    def d3_copy(k, d, half):
        swap = edge * (xh if half == 0 else 1 - xh)
        to = half + swap * (xh - half)
        return pltpu.make_async_remote_copy(
            src_ref=d3o.at[d, k, half], dst_ref=xs.at[k, (5, 3)[d], to],
            send_sem=d3_send.at[k, d, half], recv_sem=d3_recv.at[k, d, to],
            device_id=dev(xh + swap * (1 - 2 * xh), (z + (1, 7)[d]) % NZ, c, xl + swap * (1 - 2 * xl), y),
            device_id_type=MESH)

    def d4_copy(k, d):
        swap = 0 if d == 0 else edge
        to = xh if d == 0 else other + edge * (xh - other)
        return pltpu.make_async_remote_copy(
            src_ref=d4o.at[d, k], dst_ref=xs.at[k, 4, to],
            send_sem=d4_send.at[k, d], recv_sem=d4_recv.at[k, to],
            device_id=dev(xh + swap * (1 - 2 * xh), (z + (2, 6)[d]) % NZ, c, xl + swap * (1 - 2 * xl), y),
            device_id_type=MESH)

    def pass_copy(k, dz):
        return pltpu.make_async_remote_copy(
            src_ref=xs.at[k, dz, 2], dst_ref=xs.at[k, dz, xh],
            send_sem=p_send.at[k, dz], recv_sem=p_recv.at[k, dz],
            device_id=dev(pxh, z, c, pxl, y), device_id_type=MESH)

    def to_owner(k, dz, second):
        zs = (z + dz) % NZ
        y2 = zs // 2
        if second:
            half, xhd, xld = other, other + edge * (xh - other), xh + edge * (other - xh)
            hxl = xl + edge * (1 - 2 * xl)
        else:
            half, xhd, xld, hxl = xh, xh, xh, xl
        for c2 in range(2):
            src = xs.at[k, dz, half, c2]
            at = (((zs % 2) * 2 + c) * 8 + hxl * 4 + y) * 2
            dst = land.at[pl.ds(at, 2), pl.ds(k * R, R)]

            def remote():
                pltpu.make_async_remote_copy(
                    src_ref=src, dst_ref=dst, send_sem=x_send, recv_sem=l_recv,
                    device_id=dev(xhd, z, c2, xld, y2), device_id_type=MESH).start()

            if second:
                remote()
            else:
                here = is_edge & (y2 == y) & (c2 == c)

                @pl.when(here)
                def _():
                    pltpu.make_async_copy(src, dst, l_recv).start()

                pl.when(jnp.logical_not(here))(remote)

    def pick(ref, which, slot):
        idx = tbl_s[which, 0, slot]
        page = ref[jnp.maximum(idx, 0)]
        return jnp.where(idx >= 0, page, jnp.zeros_like(page))

    def extract(ref, which, k, dz):
        for half in range(2):
            swap = edge * (xh if half == 0 else 1 - xh)
            to = half + swap * (2 - half)
            for c2 in range(2):
                for r in range(2):
                    xs[k, dz, to, c2, r] = pick(ref, which, half * 32 + z * 4 + c2 * 2 + r)

        @pl.when(is_edge)
        def _():
            pass_copy(k, dz).start()

        to_owner(k, dz, False)

    def passed(k, dz):
        @pl.when(is_edge)
        def _():
            pass_copy(k, dz).wait_recv()

        to_owner(k, dz, True)

    def ev_tables():
        for e, cp in enumerate(t_copies):
            cp.wait()
            pltpu.make_async_copy(tbl_in.at[e], tbl_s.at[e + 1], tl_sem.at[e + 1]).start()
        for e in range(4):
            pltpu.make_async_copy(tbl_in.at[e], tbl_s.at[e + 1], tl_sem.at[e + 1]).wait()

    def ev_own(k):
        extract(raw[k], 0, k, 0)

    def ev_one(k):
        for d in range(2):
            raw_copy(0, k, d).wait_recv()
            raw_copy(1, k, d).start()
        if k + AHEAD < C:
            for d in range(2):
                raw_copy(0, k + AHEAD, d).start()

    def ev_one_out(k):
        for d in range(2):
            extract(ra[d][k], 1 + d, k, (7, 1)[d])

    def ev_two(k):
        for d in range(2):
            raw_copy(1, k, d).wait_recv()
            n3, n4 = ((1, 2), (7, 6))[d]
            half4 = xh if d == 0 else other
            for c2 in range(2):
                for r in range(2):
                    d4o[d, k, c2, r] = pick(rb[d][k], 3 + d, half4 * 32 + ((z + n4) % NZ) * 4 + c2 * 2 + r)
            d4_copy(k, d).start()
            for half in range(2):
                for c2 in range(2):
                    for r in range(2):
                        d3o[d, k, half, c2, r] = pick(rb[d][k], 3 + d, half * 32 + ((z + n3) % NZ) * 4 + c2 * 2 + r)
                d3_copy(k, d, half).start()

    def ev_two_out(k):
        for d in range(2):
            extract(rb[d][k], 3 + d, k, (6, 2)[d])

    def ev_pass1(k):
        for dz in (0, 7, 1):
            passed(k, dz)

    def ev_far(k):
        for dz in (6, 2):
            passed(k, dz)
        for d in range(2):
            for half in range(2):
                d3_copy_in(k, d, half)
            to_owner(k, (5, 3)[d], False)
            to_owner(k, (5, 3)[d], True)
        for half in range(2):
            d4_copy_in(k, half)
        to_owner(k, 4, False)
        to_owner(k, 4, True)

    def d3_copy_in(k, d, half):
        landed = xs.at[k, (5, 3)[d], half]
        pltpu.make_async_copy(landed, landed, d3_recv.at[k, d, half]).wait()

    def d4_copy_in(k, half):
        landed = xs.at[k, 4, half]
        pltpu.make_async_copy(landed, landed, d4_recv.at[k, half]).wait()

    scale = math.log2(math.e) / math.sqrt(HD)

    def attend(h, i):
        rows = slice(i * BQ, (i + 1) * BQ)
        keep = (lax.broadcasted_iota(jnp.int32, (BQ, BQ), 1) <= lax.broadcasted_iota(jnp.int32, (BQ, BQ), 0))
        for g in range(HG):
            cols = pl.ds(pl.multiple_of((h * HG + g) * HD, HD), HD)
            q = qbuf[rows, cols].astype(F32)
            qr = (q * cos_t[rows] + pltpu.roll(q, HD // 2, 1) * sin_t[rows]).astype(BF16)
            s_d = jnp.where(keep, dot_t(qr, krot[rows]), -1e30)
            top = jnp.max(s_d, axis=1, keepdims=True)
            if i > 0:
                s_f = dot_t(qr, krot[0:i * BQ])
                top = jnp.maximum(top, jnp.max(s_f, axis=1, keepdims=True))
            w_d = jnp.exp2((s_d - top) * scale).astype(BF16)
            out = jnp.dot(w_d, vext[rows], preferred_element_type=F32)
            if i > 0:
                w_f = jnp.exp2((s_f - top) * scale).astype(BF16)
                out = out + jnp.dot(w_f, vext[0:i * BQ], preferred_element_type=F32)
            mbuf[rows, cols] = (out[:, 0:HD] / out[:, HD:]).astype(BF16)

    own_tbl.start()
    for k in range(AHEAD):
        for d in range(2):
            raw_copy(0, k, d).start()
        if k == 0:
            for cp in t_copies:
                cp.start()
    own_tbl.wait()
    q_in.wait()

    def turn(r):
        if r < C:
            ev_one(r)
        if r == 0:
            ev_tables()
        if 0 <= r - 1 < C:
            ev_two(r - 1)
        if r < C:
            ev_own(r)
            ev_one_out(r)
        if 0 <= r - 1 < C:
            ev_pass1(r - 1)
            ev_two_out(r - 1)
        if 0 <= r - 2 < C:
            ev_far(r - 2)

    units = NH // HG * NQ
    turns = C + 2
    early = min(units, turns)

    def unit(s, carry):
        for r in range(early):
            @pl.when(s == r)
            def _():
                turn(r)
        h, i = s // NQ, s % NQ
        for j in range(NQ):
            @pl.when(i == j)
            def _():
                attend(h, j)
        return carry

    lax.fori_loop(0, units, unit, 0)
    out = pltpu.make_async_copy(mbuf, mixed_hbm, out_sem)
    out.start()
    for r in range(early, turns):
        turn(r)
    out.wait()
    for k in range(C):
        for d in range(2):
            raw_copy(0, k, d).wait_send()
            raw_copy(1, k, d).wait_send()
            d4_copy(k, d).wait_send()
            for half in range(2):
                d3_copy(k, d, half).wait_send()

        @pl.when(is_edge)
        def _():
            for dz in (0, 7, 1, 6, 2):
                pass_copy(k, dz).wait_send()
    whole = land.at[pl.ds(0, 60)]
    pltpu.make_async_copy(whole, whole, x_send).wait()

    @pl.when(jnp.logical_not(is_edge))
    def _():
        rest = land.at[pl.ds(60, 4)]
        pltpu.make_async_copy(rest, rest, x_send).wait()

    pltpu.make_async_copy(land, land, l_recv).wait()


def layout_kernel(land, mixed_in, store, mixed, lbuf, mbuf, sem, msem):
    parts = 4
    rows = T // parts
    ins, outs = [], []
    for g in range(4):
        ins.append(pltpu.make_async_copy(land.at[pl.ds(g * 16, 16)], lbuf.at[pl.ds(g * 16, 16)], sem.at[0, g]))
        ins.append(pltpu.make_async_copy(
            mixed_in.at[pl.ds(g * rows, rows)], mbuf.at[pl.ds(g * rows, rows)], msem.at[0, g]))
    for cp in ins:
        cp.start()
    for g in range(4):
        ins[2 * g].wait()
        for h in range(8):
            for r in range(2):
                outs.append(pltpu.make_async_copy(
                    lbuf.at[(g * 8 + h) * 2 + r], store.at[g * 2 + r, :, :, pl.ds(h * HD, HD)],
                    sem.at[1 + h * 2 + r, g]))
                outs[-1].start()
        ins[2 * g + 1].wait()
        outs.append(pltpu.make_async_copy(
            mbuf.at[pl.ds(g * rows, rows)], mixed.at[pl.ds(g * rows, rows)], msem.at[1, g]))
        outs[-1].start()
    for cp in outs:
        cp.wait()


def on_device(queries, keys, values, start_pages, owners):
    half = HD // 2
    inv = ROPE_THETA ** (-(np.arange(half, dtype=np.float64) * 2.0) / HD)
    inv = jnp.asarray(np.concatenate([inv, inv]).astype(np.float32).reshape(1, HD))
    anys = pl.BlockSpec(memory_space=pl.ANY)
    smem = pl.BlockSpec(memory_space=pltpu.SMEM)
    vm = lambda *s: pltpu.VMEM(s, BF16)
    dma = lambda *s: pltpu.SemaphoreType.DMA(s) if s else pltpu.SemaphoreType.DMA
    blocks = [vm(NP, R, HD)] * (5 * C)
    mixed, land = pl.pallas_call(
        main_kernel,
        out_shape=(jax.ShapeDtypeStruct((T, NH * HD), BF16), jax.ShapeDtypeStruct((64, 2 * PAGE, HD), BF16)),
        in_specs=[pl.BlockSpec(memory_space=pltpu.VMEM), smem, smem, anys, anys, anys],
        out_specs=(anys, anys),
        scratch_shapes=[
            vm(T, NH * HD), vm(T, HD), vm(T, HD), vm(T, NH * HD),
            pltpu.VMEM((T, HD), F32), pltpu.VMEM((T, HD), F32), vm(T, HD), vm(T, 2 * HD),
            pltpu.VMEM((8, 128), jnp.int32), pltpu.VMEM((4, 8, 128), jnp.int32), pltpu.SMEM((5, 8, 128), jnp.int32),
            vm(C, NZ, 3, 2, 2, R, HD), vm(2, C, 2, 2, 2, R, HD), vm(2, C, 2, 2, R, HD),
            dma(3), dma(5),
            dma(4), dma(4),
            dma(2, C, 2), dma(2, C, 2), dma(C, 2, 2), dma(C, 2, 2), dma(C, 2), dma(C, 2), dma(C, NZ), dma(C, NZ),
            dma(), dma(), dma(),
        ] + blocks,
        compiler_params=pltpu.CompilerParams(
            collective_id=0, has_side_effects=True, vmem_limit_bytes=56 << 20),
    )(inv, start_pages, owners.reshape(NP), queries, keys, values)
    store, mixed = pl.pallas_call(
        layout_kernel,
        out_shape=(jax.ShapeDtypeStruct((8, PAGE, 2, 8 * HD), BF16), jax.ShapeDtypeStruct((T, NH * HD), BF16)),
        in_specs=[anys, anys],
        out_specs=(anys, anys),
        scratch_shapes=[vm(64, PAGE, 2, HD), vm(T, NH * HD), dma(17, 4), dma(2, 4)],
        compiler_params=pltpu.CompilerParams(vmem_limit_bytes=60 << 20),
    )(land.reshape(64, PAGE, 2, HD), mixed)
    return (mixed, store)


def solution(mesh):
    return jax.shard_map(
        on_device,
        mesh=mesh,
        in_specs=(
            P("pool", "tp"),
            P("pool", "tp"),
            P("pool", "tp"),
            P("pool"),
            P("pool", None, None),
        ),
        out_specs=(P("pool", "tp"), P(("pool", "tp"), None, None, None)),
        check_vma=False,
    )
```

```python
import functools
import math

import jax
import jax.numpy as jnp
import numpy as np
from jax import lax
from jax.experimental import pallas as pl
from jax.experimental.pallas import tpu as pltpu
from jax.sharding import PartitionSpec as P

HD = 128
PAGE = 64
ROPE_THETA = 1000000.0
MESH = pl.DeviceIdType.MESH
NZ = 8
NP = 16
T = 1024
NH = 8
C = 8
AHEAD = 3
R = 2 * PAGE // C
BQ = 256
HG = 4
NQ = T // BQ
F32 = jnp.float32
BF16 = jnp.bfloat16


def dev(xh, z, c, xl, y):
    return (xh * 16 + z * 2 + c, xl * 4 + y)


def dot_t(a, b):
    return lax.dot_general(a, b, (((1,), (1,)), ((), ())), preferred_element_type=F32)


def main_kernel(inv_ref, start_ref, owners_ref, q_hbm, k_hbm, v_hbm, mixed_hbm, land, *scratch):
    (qbuf, kbuf, vbuf, mbuf, cos_t, sin_t, krot, vext, tbl, tbl_in, tbl_s,
     xs, d3o, d4o, in_sem, tl_sem, t_send, t_recv, r_send, r_recv, d3_send, d3_recv,
     d4_send, d4_recv, p_send, p_recv, x_send, l_recv, out_sem) = scratch[:29]
    blocks = scratch[29:]
    raw = blocks[0:C]
    ra = (blocks[C:2 * C], blocks[2 * C:3 * C])
    rb = (blocks[3 * C:4 * C], blocks[4 * C:5 * C])

    p_idx, t_idx = lax.axis_index("pool"), lax.axis_index("tp")
    xh, z, c = p_idx // 16, (p_idx // 2) % 8, p_idx % 2
    xl, y = t_idx // 4, t_idx % 4
    edge = 1 - (xl - xh) * (xl - xh)
    is_edge = xl == xh
    other = 1 - xh
    pxh, pxl = xh + edge * (1 - 2 * xh), xl + edge * (1 - 2 * xl)

    k_in = pltpu.make_async_copy(k_hbm, kbuf, in_sem.at[0])
    v_in = pltpu.make_async_copy(v_hbm, vbuf, in_sem.at[1])
    q_in = pltpu.make_async_copy(q_hbm, qbuf, in_sem.at[2])
    k_in.start()
    v_in.start()

    bar = pltpu.get_barrier_semaphore()

    def greet(*place):
        pl.semaphore_signal(bar, inc=1, device_id=dev(*place), device_id_type=MESH)

    for n in (1, 7, 2, 6):
        greet(xh, (z + n) % NZ, c, xl, y)

    @pl.when(is_edge)
    def _():
        for n in (0, 1, 7, 2, 6):
            greet(pxh, (z + n) % NZ, c, pxl, y)

    for half in range(2):
        xhd, xld = half + edge * (xh - half), xh + edge * (half - xh)
        for y2 in range(4):
            for c2 in range(2):
                here = is_edge & (half == xl) & (y2 == y) & (c2 == c)

                @pl.when(jnp.logical_not(here))
                def _():
                    greet(xhd, z, c2, xld, y2)

    own = [owners_ref[q] for q in range(NP)]
    lane = lax.broadcasted_iota(jnp.int32, (8, 128), 1)
    table = jnp.full((8, 128), -1, jnp.int32)
    for q in range(NP):
        rank = jnp.int32(0)
        for e in range(q):
            rank = rank + jnp.where(own[e] == own[q], 1, 0)
        table = jnp.where(lane == own[q] * 2 + rank, q, table)
    tbl[...] = table

    inv = inv_ref[...]
    base = start_ref[0] * PAGE
    page_pos = (base + PAGE * lax.broadcasted_iota(jnp.int32, (NP, HD), 0)).astype(F32)
    in_pos = lax.broadcasted_iota(jnp.int32, (PAGE, HD), 0).astype(F32)
    ang_p = page_pos * inv
    ang_i = in_pos * inv
    cos_p, sin_p, cos_i, sin_i = jnp.cos(ang_p), jnp.sin(ang_p), jnp.cos(ang_i), jnp.sin(ang_i)
    sign = jnp.where(lax.broadcasted_iota(jnp.int32, (PAGE, HD), 1) < HD // 2, -1.0, 1.0).astype(F32)
    row = lax.broadcasted_iota(jnp.int32, (2 * PAGE, 2 * PAGE), 0)
    col = lax.broadcasted_iota(jnp.int32, (2 * PAGE, 2 * PAGE), 1)
    weave = (col == (row // 2) + PAGE * (row % 2)).astype(BF16)
    k_in.wait()
    v_in.wait()
    q_in.start()
    for q in range(NP):
        rows = slice(q * PAGE, (q + 1) * PAGE)
        cos_q = cos_p[q:q + 1] * cos_i - sin_p[q:q + 1] * sin_i
        sin_q = (sin_p[q:q + 1] * cos_i + cos_p[q:q + 1] * sin_i) * sign
        cos_t[rows] = cos_q
        sin_t[rows] = sin_q
        k = kbuf[rows].astype(F32)
        kr = (k * cos_q + pltpu.roll(k, HD // 2, 1) * sin_q).astype(BF16)
        krot[rows] = kr
        v = vbuf[rows]
        both = jnp.dot(weave, jnp.concatenate([kr, v], axis=0), preferred_element_type=F32).astype(BF16)
        for k_ in range(C):
            raw[k_][q] = both[k_ * R:(k_ + 1) * R]
        vext[rows, 0:HD] = v
        vext[rows, HD:] = jnp.ones((PAGE, HD), BF16)

    pl.semaphore_wait(bar, 20 + 4 * edge)

    t_copies = []
    for e, n in enumerate((1, 7, 2, 6)):
        t_copies.append(pltpu.make_async_remote_copy(
            src_ref=tbl, dst_ref=tbl_in.at[e], send_sem=t_send.at[e], recv_sem=t_recv.at[e],
            device_id=dev(xh, (z + n) % NZ, c, xl, y), device_id_type=MESH))
    own_tbl = pltpu.make_async_copy(tbl, tbl_s.at[0], tl_sem.at[0])

    def raw_copy(stage, k, d):
        return pltpu.make_async_remote_copy(
            src_ref=raw[k] if stage == 0 else ra[d][k], dst_ref=ra[d][k] if stage == 0 else rb[d][k],
            send_sem=r_send.at[stage, k, d], recv_sem=r_recv.at[stage, k, d],
            device_id=dev(xh, (z + (1, 7)[d]) % NZ, c, xl, y), device_id_type=MESH)

    def d3_copy(k, d, half):
        swap = edge * (xh if half == 0 else 1 - xh)
        to = half + swap * (xh - half)
        return pltpu.make_async_remote_copy(
            src_ref=d3o.at[d, k, half], dst_ref=xs.at[k, (5, 3)[d], to],
            send_sem=d3_send.at[k, d, half], recv_sem=d3_recv.at[k, d, to],
            device_id=dev(xh + swap * (1 - 2 * xh), (z + (1, 7)[d]) % NZ, c, xl + swap * (1 - 2 * xl), y),
            device_id_type=MESH)

    def d4_copy(k, d):
        swap = 0 if d == 0 else edge
        to = xh if d == 0 else other + edge * (xh - other)
        return pltpu.make_async_remote_copy(
            src_ref=d4o.at[d, k], dst_ref=xs.at[k, 4, to],
            send_sem=d4_send.at[k, d], recv_sem=d4_recv.at[k, to],
            device_id=dev(xh + swap * (1 - 2 * xh), (z + (2, 6)[d]) % NZ, c, xl + swap * (1 - 2 * xl), y),
            device_id_type=MESH)

    def pass_copy(k, dz):
        return pltpu.make_async_remote_copy(
            src_ref=xs.at[k, dz, 2], dst_ref=xs.at[k, dz, xh],
            send_sem=p_send.at[k, dz], recv_sem=p_recv.at[k, dz],
            device_id=dev(pxh, z, c, pxl, y), device_id_type=MESH)

    def to_owner(k, dz, second):
        zs = (z + dz) % NZ
        y2 = zs // 2
        if second:
            half, xhd, xld = other, other + edge * (xh - other), xh + edge * (other - xh)
            hxl = xl + edge * (1 - 2 * xl)
        else:
            half, xhd, xld, hxl = xh, xh, xh, xl
        for c2 in range(2):
            src = xs.at[k, dz, half, c2]
            at = (((zs % 2) * 2 + c) * 8 + hxl * 4 + y) * 2
            dst = land.at[pl.ds(at, 2), pl.ds(k * R, R)]

            def remote():
                pltpu.make_async_remote_copy(
                    src_ref=src, dst_ref=dst, send_sem=x_send, recv_sem=l_recv,
                    device_id=dev(xhd, z, c2, xld, y2), device_id_type=MESH).start()

            if second:
                remote()
            else:
                here = is_edge & (y2 == y) & (c2 == c)

                @pl.when(here)
                def _():
                    pltpu.make_async_copy(src, dst, l_recv).start()

                pl.when(jnp.logical_not(here))(remote)

    def pick(ref, which, slot):
        idx = tbl_s[which, 0, slot]
        page = ref[jnp.maximum(idx, 0)]
        return jnp.where(idx >= 0, page, jnp.zeros_like(page))

    def extract(ref, which, k, dz):
        for half in range(2):
            swap = edge * (xh if half == 0 else 1 - xh)
            to = half + swap * (2 - half)
            for c2 in range(2):
                for r in range(2):
                    xs[k, dz, to, c2, r] = pick(ref, which, half * 32 + z * 4 + c2 * 2 + r)

        @pl.when(is_edge)
        def _():
            pass_copy(k, dz).start()

        to_owner(k, dz, False)

    def passed(k, dz):
        @pl.when(is_edge)
        def _():
            pass_copy(k, dz).wait_recv()

        to_owner(k, dz, True)

    def ev_tables():
        for e, cp in enumerate(t_copies):
            cp.wait()
            pltpu.make_async_copy(tbl_in.at[e], tbl_s.at[e + 1], tl_sem.at[e + 1]).start()
        for e in range(4):
            pltpu.make_async_copy(tbl_in.at[e], tbl_s.at[e + 1], tl_sem.at[e + 1]).wait()

    def ev_own(k):
        extract(raw[k], 0, k, 0)

    def ev_one(k):
        for d in range(2):
            raw_copy(0, k, d).wait_recv()
            raw_copy(1, k, d).start()
        if k + AHEAD < C:
            for d in range(2):
                raw_copy(0, k + AHEAD, d).start()

    def ev_one_out(k):
        for d in range(2):
            extract(ra[d][k], 1 + d, k, (7, 1)[d])

    def ev_two(k):
        for d in range(2):
            raw_copy(1, k, d).wait_recv()
            n3, n4 = ((1, 2), (7, 6))[d]
            half4 = xh if d == 0 else other
            for c2 in range(2):
                for r in range(2):
                    d4o[d, k, c2, r] = pick(rb[d][k], 3 + d, half4 * 32 + ((z + n4) % NZ) * 4 + c2 * 2 + r)
            d4_copy(k, d).start()
            for half in range(2):
                for c2 in range(2):
                    for r in range(2):
                        d3o[d, k, half, c2, r] = pick(rb[d][k], 3 + d, half * 32 + ((z + n3) % NZ) * 4 + c2 * 2 + r)
                d3_copy(k, d, half).start()

    def ev_two_out(k):
        for d in range(2):
            extract(rb[d][k], 3 + d, k, (6, 2)[d])

    def ev_pass1(k):
        for dz in (0, 7, 1):
            passed(k, dz)

    def ev_far(k):
        for dz in (6, 2):
            passed(k, dz)
        for d in range(2):
            for half in range(2):
                d3_copy_in(k, d, half)
            to_owner(k, (5, 3)[d], False)
            to_owner(k, (5, 3)[d], True)
        for half in range(2):
            d4_copy_in(k, half)
        to_owner(k, 4, False)
        to_owner(k, 4, True)

    def d3_copy_in(k, d, half):
        landed = xs.at[k, (5, 3)[d], half]
        pltpu.make_async_copy(landed, landed, d3_recv.at[k, d, half]).wait()

    def d4_copy_in(k, half):
        landed = xs.at[k, 4, half]
        pltpu.make_async_copy(landed, landed, d4_recv.at[k, half]).wait()

    scale = math.log2(math.e) / math.sqrt(HD)

    def attend(h, i):
        rows = slice(i * BQ, (i + 1) * BQ)
        keep = (lax.broadcasted_iota(jnp.int32, (BQ, BQ), 1) <= lax.broadcasted_iota(jnp.int32, (BQ, BQ), 0))
        for g in range(HG):
            cols = pl.ds(pl.multiple_of((h * HG + g) * HD, HD), HD)
            q = qbuf[rows, cols].astype(F32)
            qr = (q * cos_t[rows] + pltpu.roll(q, HD // 2, 1) * sin_t[rows]).astype(BF16)
            s_d = jnp.where(keep, dot_t(qr, krot[rows]), -1e30)
            top = jnp.max(s_d, axis=1, keepdims=True)
            if i > 0:
                s_f = dot_t(qr, krot[0:i * BQ])
                top = jnp.maximum(top, jnp.max(s_f, axis=1, keepdims=True))
            w_d = jnp.exp2((s_d - top) * scale).astype(BF16)
            out = jnp.dot(w_d, vext[rows], preferred_element_type=F32)
            if i > 0:
                w_f = jnp.exp2((s_f - top) * scale).astype(BF16)
                out = out + jnp.dot(w_f, vext[0:i * BQ], preferred_element_type=F32)
            mbuf[rows, cols] = (out[:, 0:HD] / out[:, HD:]).astype(BF16)

    own_tbl.start()
    for k in range(AHEAD):
        for d in range(2):
            raw_copy(0, k, d).start()
        if k == 0:
            for cp in t_copies:
                cp.start()
    own_tbl.wait()
    q_in.wait()

    def turn(r):
        if r < C:
            ev_one(r)
        if r == 0:
            ev_tables()
        if 0 <= r - 1 < C:
            ev_two(r - 1)
        if r < C // 2:
            ev_own(2 * r)
            ev_own(2 * r + 1)
        if r < C:
            ev_one_out(r)
        if 0 <= r - 1 < C:
            ev_pass1(r - 1)
            ev_two_out(r - 1)
        if 0 <= r - 2 < C:
            ev_far(r - 2)

    units = NH // HG * NQ
    turns = C + 2
    early = min(units, turns)

    def unit(s, carry):
        for r in range(early):
            @pl.when(s == r)
            def _():
                turn(r)
        h, i = s // NQ, s % NQ
        for j in range(NQ):
            @pl.when(i == j)
            def _():
                attend(h, j)
        return carry

    lax.fori_loop(0, units, unit, 0)
    out = pltpu.make_async_copy(mbuf, mixed_hbm, out_sem)
    out.start()
    for r in range(early, turns):
        turn(r)
    out.wait()
    for k in range(C):
        for d in range(2):
            raw_copy(0, k, d).wait_send()
            raw_copy(1, k, d).wait_send()
            d4_copy(k, d).wait_send()
            for half in range(2):
                d3_copy(k, d, half).wait_send()

        @pl.when(is_edge)
        def _():
            for dz in (0, 7, 1, 6, 2):
                pass_copy(k, dz).wait_send()
    whole = land.at[pl.ds(0, 60)]
    pltpu.make_async_copy(whole, whole, x_send).wait()

    @pl.when(jnp.logical_not(is_edge))
    def _():
        rest = land.at[pl.ds(60, 4)]
        pltpu.make_async_copy(rest, rest, x_send).wait()

    pltpu.make_async_copy(land, land, l_recv).wait()


def layout_kernel(land, mixed_in, store, mixed, lbuf, mbuf, sem, msem):
    parts = 4
    rows = T // parts
    ins, outs = [], []
    for g in range(4):
        ins.append(pltpu.make_async_copy(land.at[pl.ds(g * 16, 16)], lbuf.at[pl.ds(g * 16, 16)], sem.at[0, g]))
        ins.append(pltpu.make_async_copy(
            mixed_in.at[pl.ds(g * rows, rows)], mbuf.at[pl.ds(g * rows, rows)], msem.at[0, g]))
    for cp in ins:
        cp.start()
    for g in range(4):
        ins[2 * g].wait()
        for h in range(8):
            for r in range(2):
                outs.append(pltpu.make_async_copy(
                    lbuf.at[(g * 8 + h) * 2 + r], store.at[g * 2 + r, :, :, pl.ds(h * HD, HD)],
                    sem.at[1 + h * 2 + r, g]))
                outs[-1].start()
        ins[2 * g + 1].wait()
        outs.append(pltpu.make_async_copy(
            mbuf.at[pl.ds(g * rows, rows)], mixed.at[pl.ds(g * rows, rows)], msem.at[1, g]))
        outs[-1].start()
    for cp in outs:
        cp.wait()


def on_device(queries, keys, values, start_pages, owners):
    half = HD // 2
    inv = ROPE_THETA ** (-(np.arange(half, dtype=np.float64) * 2.0) / HD)
    inv = jnp.asarray(np.concatenate([inv, inv]).astype(np.float32).reshape(1, HD))
    anys = pl.BlockSpec(memory_space=pl.ANY)
    smem = pl.BlockSpec(memory_space=pltpu.SMEM)
    vm = lambda *s: pltpu.VMEM(s, BF16)
    dma = lambda *s: pltpu.SemaphoreType.DMA(s) if s else pltpu.SemaphoreType.DMA
    blocks = [vm(NP, R, HD)] * (5 * C)
    mixed, land = pl.pallas_call(
        main_kernel,
        out_shape=(jax.ShapeDtypeStruct((T, NH * HD), BF16), jax.ShapeDtypeStruct((64, 2 * PAGE, HD), BF16)),
        in_specs=[pl.BlockSpec(memory_space=pltpu.VMEM), smem, smem, anys, anys, anys],
        out_specs=(anys, anys),
        scratch_shapes=[
            vm(T, NH * HD), vm(T, HD), vm(T, HD), vm(T, NH * HD),
            pltpu.VMEM((T, HD), F32), pltpu.VMEM((T, HD), F32), vm(T, HD), vm(T, 2 * HD),
            pltpu.VMEM((8, 128), jnp.int32), pltpu.VMEM((4, 8, 128), jnp.int32), pltpu.SMEM((5, 8, 128), jnp.int32),
            vm(C, NZ, 3, 2, 2, R, HD), vm(2, C, 2, 2, 2, R, HD), vm(2, C, 2, 2, R, HD),
            dma(3), dma(5),
            dma(4), dma(4),
            dma(2, C, 2), dma(2, C, 2), dma(C, 2, 2), dma(C, 2, 2), dma(C, 2), dma(C, 2), dma(C, NZ), dma(C, NZ),
            dma(), dma(), dma(),
        ] + blocks,
        compiler_params=pltpu.CompilerParams(
            collective_id=0, has_side_effects=True, vmem_limit_bytes=56 << 20),
    )(inv, start_pages, owners.reshape(NP), queries, keys, values)
    store, mixed = pl.pallas_call(
        layout_kernel,
        out_shape=(jax.ShapeDtypeStruct((8, PAGE, 2, 8 * HD), BF16), jax.ShapeDtypeStruct((T, NH * HD), BF16)),
        in_specs=[anys, anys],
        out_specs=(anys, anys),
        scratch_shapes=[vm(64, PAGE, 2, HD), vm(T, NH * HD), dma(17, 4), dma(2, 4)],
        compiler_params=pltpu.CompilerParams(vmem_limit_bytes=60 << 20),
    )(land.reshape(64, PAGE, 2, HD), mixed)
    return (mixed, store)


def solution(mesh):
    return jax.shard_map(
        on_device,
        mesh=mesh,
        in_specs=(
            P("pool", "tp"),
            P("pool", "tp"),
            P("pool", "tp"),
            P("pool"),
            P("pool", None, None),
        ),
        out_specs=(P("pool", "tp"), P(("pool", "tp"), None, None, None)),
        check_vma=False,
    )
```
